32 devices in a mesh: seq: 4 (over y, x), ctx: 8 (over z, core).
Axes of the slice: x: 2, y: 2, z: 4, core: 2. Of those that a mesh axis runs over, the one named last changes fastest.
Arguments:
- delta_query: bfloat16 [4, 1024, 2048], P('seq', 'ctx'), may hold values from -6 to 6
- delta_key: bfloat16 [4, 1024, 2048], P('seq', 'ctx'), may hold values from -6 to 6
- delta_value: bfloat16 [4, 1024, 4096], P('seq', 'ctx'), may hold values from -6 to 6
- delta_gate: bfloat16 [4, 1024, 4096], P('seq', 'ctx'), may hold values from -6 to 6
- delta_beta: float32 [4, 32, 1024], P('seq', None, 'ctx'), may hold values from 0 to 1
- delta_decay: float32 [4, 32, 1024], P('seq', None, 'ctx'), may hold values from -2 to 0
- norm_gain: float32 [128], replicated, may hold values from 0.5 to 1.5
- attention_query: bfloat16 [4, 1024, 4096], P('seq', 'ctx'), may hold values from -4 to 4
- attention_key_value: bfloat16 [4, 1024, 1024], P('seq', 'ctx'), may hold values from -4 to 4
- attention_gate: bfloat16 [4, 1024, 4096], P('seq', 'ctx'), may hold values from -6 to 6
- moe_input: bfloat16 [4, 1024, 2048], P('seq', 'ctx'), may hold values from -6 to 6
- routes: int32 [4, 1024, 10], P('seq', 'ctx'), may hold values from 0 to 31, all different within a row; in each aligned block of 128 rows (0 to 127, 128 to 255, ..., all dimensions but the last counted through in order) at most 64 rows name the same one
- drop_mask: int32 [4, 1024, 10], P('seq', 'ctx'), may hold values 0 or 1
- route_weights: float32 [4, 1024, 10], P('seq', 'ctx'), may hold values from 0.05 to 0.5
- w_gate: bfloat16 [32, 2048, 512], P(('seq', 'ctx')), may hold values from -0.125 to 0.125
- w_up: bfloat16 [32, 2048, 512], P(('seq', 'ctx')), may hold values from -0.125 to 0.125
- w_down: bfloat16 [32, 512, 2048], P(('seq', 'ctx')), may hold values from -0.25 to 0.25
Outputs:
- delta_out: bfloat16 [4, 1024, 4096], P('seq', 'ctx')
- attn_out: bfloat16 [4, 1024, 4096], P('seq', 'ctx')
- moe_out: bfloat16 [4, 1024, 2048], P('seq', 'ctx')
The draws below stay inside these ranges and needn't reach their ends.
Inputs may be any that keep to these rules, and one draw needn't show every extreme that they name: `routes`: within the rows of one device (aligned blocks of 128 positions), each token names 10 different experts and no expert is named more than 64 times; in some block some expert is named exactly 64 times. `drop_mask`: 1 keeps the chosen expert, 0 drops it.
All inputs are finite; a program needn't handle non-finite values. No bound on the sum of `drop_mask` on one device may be relied on, other than what follows from the above.
Results may differ from the reference program's by a relative error of at most 0.011.
Values may be sent and summed in bfloat16 or wider, within the bound.
A program may use at most 384 MiB of HBM per device.

```python
import math
import jax
import jax.numpy as jnp
import numpy as np
from jax import lax

D = 2048
HV = 32
HKD = 16
DK = 128
DV = 128
QUERY_HEADS = 16
KEY_VALUE_HEADS = 2
HEAD_WIDTH = 256
FFE = 512
TOP = 10
SPAN = 64
LOCAL_TOKENS = 128
SEQUENCE_COUNT = 4
SEQUENCE_LENGTH = 1024
EXPERTS = 32
CAP = 64


def head_classes(key):
    share = 0.5
    return jax.random.uniform(key, (SEQUENCE_COUNT, HV, 1)) < share


def log_uniform(key, shape, lower, upper):
    return jnp.exp(jax.random.uniform(key, shape, jnp.float32, math.log(lower), math.log(upper)))


def draw_delta_decay(key, part):
    slow = head_classes(jax.random.fold_in(key, 3))
    slow_rate = log_uniform(jax.random.fold_in(key, 31), (SEQUENCE_COUNT, HV, 1), 0.05, 0.3) / SEQUENCE_LENGTH
    fast_rate = log_uniform(jax.random.fold_in(key, 32), (SEQUENCE_COUNT, HV, 1), 1.0 / 50.0, 1.0 / 30.0)
    head_rate = jnp.where(slow, slow_rate, fast_rate)
    block_list = SEQUENCE_LENGTH // LOCAL_TOKENS
    device_factor = log_uniform(jax.random.fold_in(key, 33), (SEQUENCE_COUNT, HV, block_list, 1), 0.5, 2.0)
    token_factor = jax.random.uniform(jax.random.fold_in(key, 34), (SEQUENCE_COUNT, HV, block_list, LOCAL_TOKENS), jnp.float32, 0.5, 1.5)
    rate_values = (head_rate[:, :, :, None] * device_factor * token_factor).reshape(SEQUENCE_COUNT, HV, SEQUENCE_LENGTH)
    surge_position = jax.random.randint(jax.random.fold_in(key, 35), (SEQUENCE_COUNT, 3), 0, SEQUENCE_LENGTH)
    surge_depth = jax.random.uniform(jax.random.fold_in(key, 36), (SEQUENCE_COUNT, 3), jnp.float32, 0.2, 0.35)
    place_list = jnp.arange(SEQUENCE_LENGTH, dtype=jnp.int32)
    surge_list = jnp.sum(jnp.where(place_list[None, None, :] == surge_position[:, :, None], jnp.log(1.0 - surge_depth)[:, :, None], 0.0), axis=1)
    return (surge_list[:, None, :] - rate_values).astype(jnp.float32)


def draw_delta_beta(key, part):
    slow = head_classes(jax.random.fold_in(key, 3))
    slow_beta = log_uniform(jax.random.fold_in(key, 41), (SEQUENCE_COUNT, HV, SEQUENCE_LENGTH), 0.003, 0.03)
    fast_beta = jax.random.uniform(jax.random.fold_in(key, 42), (SEQUENCE_COUNT, HV, SEQUENCE_LENGTH), jnp.float32, 0.1, 0.9)
    return jnp.where(slow, slow_beta, fast_beta).astype(jnp.float32)


def draw_attention_query(key, part):
    value_rows = jnp.clip(jax.random.normal(jax.random.fold_in(key, 11), (SEQUENCE_COUNT, SEQUENCE_LENGTH, QUERY_HEADS * HEAD_WIDTH)), -4.0, 4.0)
    return value_rows.astype(jnp.bfloat16)


def draw_attention_key_value(key, part):
    value_rows = jnp.clip(jax.random.normal(jax.random.fold_in(key, 12), (SEQUENCE_COUNT, SEQUENCE_LENGTH, 2 * KEY_VALUE_HEADS * HEAD_WIDTH)), -4.0, 4.0)
    return value_rows.astype(jnp.bfloat16)


def set_ends(values, own_key, least, top_value):
    longest = values.shape.index(max(values.shape))
    spots = []
    for shift in (0, 1):
        where = [jax.random.randint(jax.random.fold_in(own_key, axis), (), 0, length) for axis, length in enumerate(values.shape)]
        where[longest] = (where[longest] + shift) % values.shape[longest]
        spots.append(tuple(where))
    return values.at[spots[0]].set(least).at[spots[1]].set(top_value)


def block_scale(stream_key, extent, cuts, low, top_value):
    def one(dim, parts):
        steps = jax.random.uniform(jax.random.fold_in(jax.random.fold_in(stream_key, 6), dim), (parts,), jnp.float32, low / len(cuts), top_value / len(cuts))
        return jnp.repeat(jnp.exp(steps), extent[dim] // parts).reshape((-1,) + (1,) * (len(extent) - dim - 1))

    gain = one(*cuts[0])
    for cut in cuts[1:]:
        gain = gain * one(*cut)
    return gain


def routed_block(key, own, number, rows, number_of, top, bound, skew):
    ranking = jax.random.permutation(key, number_of)
    heavy_load, common = shares(number_of, rows * top, bound, skew, True), shares(number_of, rows * top, bound, skew, False)
    places = jnp.arange(number_of)

    def named(lengths, offset_by):
        used = int((lengths > 0).sum())
        fixed = max(1, used // 4)
        moved = fixed + (places - fixed + offset_by * (used - fixed)) % max(1, number_of - fixed)
        return jnp.zeros((number_of,), jnp.int32).at[ranking[jnp.where(places < fixed, places, moved)]].set(jnp.asarray(lengths, jnp.int32))

    lengths = jnp.where(number % 4 == 0, named(heavy_load, number // 4), named(common, number - number // 4 - 1))
    mixed = jax.random.permutation(jax.random.fold_in(own, 3), number_of)
    giver, receiver = mixed[0:number_of // 2 * 2:2], mixed[1:number_of // 2 * 2:2]
    margin = jnp.minimum(lengths[giver] - 1, bound - lengths[receiver]) // 2
    margin = jnp.where((giver == ranking[0]) | (receiver == ranking[0]) | (lengths[receiver] == 0), 0, jnp.maximum(margin, 0))
    moved = jax.random.randint(jax.random.fold_in(own, 4), (number_of // 2,), 0, 1 << 20) % (margin + 1)
    lengths = lengths.at[giver].add(-moved).at[receiver].add(moved)
    items = jnp.searchsorted(jnp.cumsum(lengths), jnp.arange(rows * top), side="right").astype(jnp.int32)
    grid = items.reshape(top, rows).T
    grid = grid[jax.random.permutation(jax.random.fold_in(own, 1), rows)]
    offset_by = jax.random.randint(jax.random.fold_in(own, 2), (rows, 1), 0, top)
    return jnp.take_along_axis(grid, (jnp.arange(top)[None, :] + offset_by) % top, axis=1)


def shares(number_of, total, limit, skew, full):
    weights = [(1 << 20) // math.isqrt(grade ** skew) + 1 for grade in range(1, number_of + 1)]
    largest = limit if full else min(limit, max(-(-total // number_of), total * weights[0] // sum(weights)))
    least = 1 if total - largest >= number_of - 1 else 0
    counts, rest = [largest] + [least] * (number_of - 1), total - largest - least * (number_of - 1)
    while rest > 0:
        candidates = [i for i in range(1, number_of) if counts[i] < largest] or [i for i in range(1, number_of) if counts[i] < limit]
        pool, remaining = sum([weights[i] for i in candidates]), rest
        for i in candidates:
            more = min(limit - counts[i], max(1, remaining * weights[i] // pool), rest)
            counts[i] = counts[i] + more
            rest = rest - more
    return np.array(counts)


def gaussian(stream_key, shape, scale, reach, shards=(), kind=jnp.bfloat16):
    values = scale * jax.random.normal(stream_key, shape, jnp.float32)
    if shards:
        values = values * block_scale(stream_key, shape, shards, -0.22, 0.18)
    return jnp.clip(values, -reach, reach).astype(kind)


def setup_inputs(seed: int = 0) -> dict:
    key_list = jax.random.split(jax.random.key(seed), 18)
    delta_query = gaussian(key_list[0], (SEQUENCE_COUNT, SEQUENCE_LENGTH, HKD * DK), 1.0, 6.0, ((0, 4), (1, 8)))
    delta_key = gaussian(key_list[1], (SEQUENCE_COUNT, SEQUENCE_LENGTH, HKD * DK), 1.0, 6.0, ((0, 4), (1, 8)))
    delta_value = gaussian(key_list[2], (SEQUENCE_COUNT, SEQUENCE_LENGTH, HV * DV), 1.0, 6.0, ((0, 4), (1, 8)))
    delta_gate = gaussian(key_list[3], (SEQUENCE_COUNT, SEQUENCE_LENGTH, HV * DV), 1.0, 6.0, ((0, 4), (1, 8)))
    delta_beta = draw_delta_beta(jax.random.fold_in(key_list[17], 71), 0)
    delta_decay = draw_delta_decay(jax.random.fold_in(key_list[17], 71), 0)
    norm_gain = jnp.clip(1.0 + 0.1 * jax.random.normal(key_list[6], (DV,), jnp.float32), 0.5, 1.5)
    attention_query = draw_attention_query(jax.random.fold_in(key_list[17], 71), 0)
    attention_key_value = draw_attention_key_value(jax.random.fold_in(key_list[17], 71), 0)
    attention_gate = gaussian(key_list[9], (SEQUENCE_COUNT, SEQUENCE_LENGTH, QUERY_HEADS * HEAD_WIDTH), 1.0, 6.0, ((0, 4), (1, 8)))
    moe_input = gaussian(key_list[10], (SEQUENCE_COUNT, SEQUENCE_LENGTH, D), 1.0, 6.0, ((0, 4), (1, 8)))
    routes_keys = jax.random.split(jax.random.fold_in(key_list[11], 1), SEQUENCE_COUNT * SEQUENCE_LENGTH // LOCAL_TOKENS)
    routes_turns = jax.random.permutation(jax.random.fold_in(key_list[11], 3), SEQUENCE_COUNT * SEQUENCE_LENGTH // LOCAL_TOKENS)
    routes = jax.vmap(lambda own, number: routed_block(jax.random.fold_in(key_list[11], 2), own, number, LOCAL_TOKENS, EXPERTS, TOP, CAP, 1))(routes_keys, routes_turns).reshape((SEQUENCE_COUNT, SEQUENCE_LENGTH, TOP))
    drop_mask = set_ends((jax.random.randint(key_list[12], (SEQUENCE_COUNT, SEQUENCE_LENGTH, TOP), 0, 4) < 3).astype(jnp.int32), jax.random.fold_in(key_list[12], 1), 0, 1)
    route_weights = jnp.clip(jnp.exp(math.log(0.5) - 2.3025851 * jax.random.uniform(key_list[13], (SEQUENCE_COUNT, SEQUENCE_LENGTH, TOP), jnp.float32) ** block_scale(key_list[13], (SEQUENCE_COUNT, SEQUENCE_LENGTH, TOP), ((0, 4), (1, 8)), -0.2, 0.2)), 0.05, 0.5)
    w_gate = gaussian(key_list[14], (EXPERTS, D, FFE), D ** -0.5, 0.125, ((0, 32),))
    w_up = gaussian(key_list[15], (EXPERTS, D, FFE), D ** -0.5, 0.125, ((0, 32),))
    w_down = gaussian(key_list[16], (EXPERTS, FFE, D), FFE ** -0.5, 0.25, ((0, 32),))
    return {"delta_query": delta_query, "delta_key": delta_key, "delta_value": delta_value, "delta_gate": delta_gate, "delta_beta": delta_beta, "delta_decay": delta_decay, "norm_gain": norm_gain, "attention_query": attention_query, "attention_key_value": attention_key_value, "attention_gate": attention_gate, "moe_input": moe_input, "routes": routes, "drop_mask": drop_mask, "route_weights": route_weights, "w_gate": w_gate, "w_up": w_up, "w_down": w_down}


precise = lax.Precision.HIGHEST

def unit_rows(matrix):
    return matrix / jnp.sqrt(lax.optimization_barrier(jnp.sum(matrix * matrix, axis=-1, keepdims=True)) + 1e-06)

def span_terms(query_rows, keys, value_rows, beta, decay):
    size = decay.shape[-1]
    key_dim = keys.shape[-1]
    value_dim = value_rows.shape[-1]
    cumulative = jnp.cumsum(decay, axis=-1)
    place_list = jnp.arange(size)
    lower = place_list[:, None] >= place_list[None, :]
    strict = place_list[:, None] > place_list[None, :]
    spread = cumulative[..., :, None] - cumulative[..., None, :]
    decay_ratio = jnp.exp(jnp.where(lower, spread, -1e+30))
    key_key = jnp.einsum('...ik,...jk->...ij', keys, keys, precision=precise)
    query_key = jnp.einsum('...ik,...jk->...ij', query_rows, keys, precision=precise)
    system = jnp.eye(size, dtype=jnp.float32) + jnp.where(strict, beta[..., :, None] * decay_ratio * key_key, 0.0)
    retained = jnp.exp(cumulative)
    right_side = jnp.concatenate([beta[..., None] * value_rows, (beta * retained)[..., None] * keys], axis=-1)
    solved = jax.scipy.linalg.solve_triangular(system, right_side, lower=True, unit_diagonal=True)
    new_values = solved[..., :value_dim]
    new_keys = solved[..., value_dim:]
    mixing = decay_ratio * query_key
    query_eff = retained[..., None] * query_rows - jnp.einsum('...ij,...jk->...ik', mixing, new_keys, precision=precise)
    direct = jnp.einsum('...ij,...jv->...iv', mixing, new_values, precision=precise)
    tail_keys = jnp.exp(cumulative[..., -1:] - cumulative)[..., None] * keys
    carry_a = retained[..., -1:, None] * jnp.eye(key_dim, dtype=jnp.float32) - jnp.einsum('...ck,...cl->...kl', new_keys, tail_keys, precision=precise)
    carry_b = jnp.einsum('...cv,...cl->...vl', new_values, tail_keys, precision=precise)
    return (query_eff, direct, carry_a, carry_b)

def gated_norm(outputs, delta_gate, norm_gain):
    scale = lax.rsqrt(lax.optimization_barrier(jnp.mean(outputs * outputs, axis=-1, keepdims=True)) + 1e-06)
    gate_vals = delta_gate.astype(jnp.float32).reshape(outputs.shape)
    normed = outputs * scale * norm_gain * jax.nn.silu(gate_vals)
    return normed.astype(jnp.bfloat16).reshape(delta_gate.shape)

def delta_layer(delta_query, delta_key, delta_value, delta_gate, delta_beta, delta_decay, norm_gain):
    head_repeat = HV // HKD
    n_spans = SEQUENCE_LENGTH // SPAN
    query_rows = unit_rows(delta_query.astype(jnp.float32).reshape(SEQUENCE_COUNT, SEQUENCE_LENGTH, HKD, DK)) * (1.0 / math.sqrt(DK))
    query_rows = jnp.repeat(query_rows, head_repeat, axis=2)
    keys = jnp.repeat(unit_rows(delta_key.astype(jnp.float32).reshape(SEQUENCE_COUNT, SEQUENCE_LENGTH, HKD, DK)), head_repeat, axis=2)
    value_rows = delta_value.astype(jnp.float32).reshape(SEQUENCE_COUNT, SEQUENCE_LENGTH, HV, DV)

    def to_spans(array):
        return array.reshape(SEQUENCE_COUNT, n_spans, SPAN, HV, array.shape[-1]).transpose(1, 0, 3, 2, 4)

    def gate_spans(array):
        return array.reshape(SEQUENCE_COUNT, HV, n_spans, SPAN).transpose(2, 0, 1, 3)

    def advance(state, pieces):
        query_eff, direct, carry_a, carry_b = span_terms(*pieces)
        output = jnp.einsum('shck,shvk->shcv', query_eff, state, precision=precise) + direct
        state = jnp.einsum('shvk,shkl->shvl', state, carry_a, precision=precise) + carry_b
        return (state, output)
    start = jnp.zeros((SEQUENCE_COUNT, HV, DV, DK), jnp.float32)
    pieces = (to_spans(query_rows), to_spans(keys), to_spans(value_rows), gate_spans(delta_beta), gate_spans(delta_decay))
    final_state, outputs = lax.scan(advance, start, pieces)
    outputs = outputs.transpose(1, 0, 3, 2, 4).reshape(SEQUENCE_COUNT, SEQUENCE_LENGTH, HV, DV)
    return gated_norm(outputs, delta_gate, norm_gain)

def attention_layer(attention_query, attention_key_value, attention_gate):
    block_list = SEQUENCE_LENGTH // LOCAL_TOKENS
    head_groups = QUERY_HEADS // KEY_VALUE_HEADS
    query_rows = attention_query.reshape(SEQUENCE_COUNT, block_list, LOCAL_TOKENS, KEY_VALUE_HEADS, head_groups, HEAD_WIDTH)
    key_value = attention_key_value.reshape(SEQUENCE_COUNT, block_list, LOCAL_TOKENS, 2, KEY_VALUE_HEADS, HEAD_WIDTH)
    previous = jnp.concatenate([jnp.zeros_like(key_value[:, :1]), key_value[:, :-1]], axis=1)
    window = jnp.concatenate([previous, key_value], axis=2)
    gate_values = attention_gate.reshape(SEQUENCE_COUNT, block_list, LOCAL_TOKENS, KEY_VALUE_HEADS, head_groups, HEAD_WIDTH)
    starts = jnp.arange(block_list, dtype=jnp.int32) * LOCAL_TOKENS

    def one_block(pieces):
        query_block, window_block, gate_block, base = pieces
        scores = jnp.einsum('stkgd,sukd->skgtu', query_block.astype(jnp.float32), window_block[:, :, 0].astype(jnp.float32), precision=precise) * (1.0 / math.sqrt(HEAD_WIDTH))
        query_pos = base + jnp.arange(LOCAL_TOKENS, dtype=jnp.int32)
        key_pos = base - LOCAL_TOKENS + jnp.arange(2 * LOCAL_TOKENS, dtype=jnp.int32)
        visible = (key_pos[None, :] <= query_pos[:, None]) & (key_pos[None, :] > query_pos[:, None] - LOCAL_TOKENS) & (key_pos[None, :] >= 0)
        scores = jnp.where(visible, scores, -jnp.inf)
        row_max = lax.optimization_barrier(jnp.max(scores, axis=-1, keepdims=True))
        lifted = jnp.exp(scores - row_max)
        probs = (lifted / lax.optimization_barrier(jnp.sum(lifted, axis=-1, keepdims=True))).astype(jnp.bfloat16)
        mixed = jnp.einsum('skgtu,sukd->stkgd', probs.astype(jnp.float32), window_block[:, :, 1].astype(jnp.float32), precision=precise)
        gated = mixed * jax.nn.sigmoid(gate_block.astype(jnp.float32))
        return gated.astype(jnp.bfloat16).reshape(SEQUENCE_COUNT, LOCAL_TOKENS, QUERY_HEADS * HEAD_WIDTH)
    outputs = lax.map(one_block, (jnp.moveaxis(query_rows, 1, 0), jnp.moveaxis(window, 1, 0), jnp.moveaxis(gate_values, 1, 0), starts))
    return outputs.transpose(1, 0, 2, 3).reshape(SEQUENCE_COUNT, SEQUENCE_LENGTH, QUERY_HEADS * HEAD_WIDTH)

def slot_numbers(expert_ids, experts):
    onehot = (expert_ids[:, None] == jnp.arange(experts, dtype=jnp.int32)[None, :]).astype(jnp.int32)
    earlier = jnp.cumsum(onehot, axis=0) - onehot
    return lax.optimization_barrier(jnp.sum(earlier * onehot, axis=1)).astype(jnp.int32)

def expert_layer(moe_input, routes, drop_mask, route_weights, w_gate, w_up, w_down):
    blocks_all = SEQUENCE_COUNT * (SEQUENCE_LENGTH // LOCAL_TOKENS)
    per_block = LOCAL_TOKENS * TOP
    flat_routes = routes.reshape(blocks_all, per_block).astype(jnp.int32)
    slots = jax.vmap(lambda ids: slot_numbers(ids, EXPERTS))(flat_routes)
    sources = jnp.broadcast_to(jnp.arange(blocks_all, dtype=jnp.int32)[:, None], (blocks_all, per_block))
    tokens = sources * LOCAL_TOKENS + (jnp.arange(per_block, dtype=jnp.int32) // TOP)[None, :]
    keep_flags = drop_mask.reshape(blocks_all, per_block)
    weights = keep_flags.astype(jnp.float32) * route_weights.reshape(blocks_all, per_block)
    table_tok = jnp.zeros((EXPERTS, blocks_all, CAP), jnp.int32).at[flat_routes, sources, slots].set(tokens)
    table_keep = jnp.zeros((EXPERTS, blocks_all, CAP), jnp.int32).at[flat_routes, sources, slots].set(keep_flags)
    table_weight = jnp.zeros((EXPERTS, blocks_all, CAP), jnp.float32).at[flat_routes, sources, slots].set(weights)
    tokens_flat = moe_input.reshape(-1, D)

    def per_expert(total, pieces):
        tok_ids, keep_ids, weight_ids, gate_w, up_w, down_w = pieces
        flat_ids = tok_ids.reshape(-1)
        rows = tokens_flat[flat_ids] * keep_ids.reshape(-1, 1).astype(jnp.bfloat16)
        gate_part = jnp.dot(rows.astype(jnp.float32), gate_w.astype(jnp.float32), preferred_element_type=jnp.float32)
        up_part = jnp.dot(rows.astype(jnp.float32), up_w.astype(jnp.float32), preferred_element_type=jnp.float32)
        hidden = (jax.nn.silu(gate_part) * up_part).astype(jnp.bfloat16)
        result = jnp.dot(hidden.astype(jnp.float32), down_w.astype(jnp.float32), preferred_element_type=jnp.float32).astype(jnp.bfloat16)
        total = total.at[flat_ids].add(weight_ids.reshape(-1, 1) * result.astype(jnp.float32))
        return (total, None)
    start = jnp.zeros((blocks_all * LOCAL_TOKENS, D), jnp.float32)
    total, unused = lax.scan(per_expert, start, (table_tok, table_keep, table_weight, w_gate, w_up, w_down))
    return total.astype(jnp.bfloat16).reshape(SEQUENCE_COUNT, SEQUENCE_LENGTH, D)

def reference(delta_query, delta_key, delta_value, delta_gate, delta_beta, delta_decay, norm_gain, attention_query, attention_key_value, attention_gate, moe_input, routes, drop_mask, route_weights, w_gate, w_up, w_down):
    delta_out = delta_layer(delta_query, delta_key, delta_value, delta_gate, delta_beta, delta_decay, norm_gain)
    attn_out = attention_layer(attention_query, attention_key_value, attention_gate)
    moe_out = expert_layer(moe_input, routes, drop_mask, route_weights, w_gate, w_up, w_down)
    return (delta_out, attn_out, moe_out)
```

```python
import functools
import math

import jax
import jax.numpy as jnp
from jax import lax
from jax.experimental import pallas as pl
from jax.experimental.pallas import tpu as pltpu
from jax.sharding import PartitionSpec as P

HV = 32
HKD = 16
DK = 128
DV = 128
QUERY_HEADS = 16
KEY_VALUE_HEADS = 2
HEAD_WIDTH = 256
PACK = DV + DK + 16
F32 = jnp.float32
BF16 = jnp.bfloat16
VMEM = 50 * 1024 * 1024


def halves(a):
    high = a.astype(BF16)
    return high, (a - high.astype(F32)).astype(BF16)


def mm(a, b):
    return jnp.dot(a, b, preferred_element_type=F32)


def mm_nt(a, b):
    return lax.dot_general(a, b, (((1,), (1,)), ((), ())), preferred_element_type=F32)


def mm_tn(a, b):
    return lax.dot_general(a, b, (((0,), (0,)), ((), ())), preferred_element_type=F32)


def mm_square(a, b):
    a_high, a_low = halves(a)
    b_high, b_low = halves(b)
    row = jnp.concatenate([b_high, b_low], axis=1)
    both = mm(jnp.concatenate([a_high, a_low], axis=1), jnp.concatenate([row, row], axis=0))
    width = b.shape[1]
    return both[:, :width] + both[:, width:]


def column(row, size):
    return jnp.broadcast_to(row, (size, row.shape[1])).T


def unit_scale(rows):
    return 1.0 / jnp.sqrt(jnp.sum(rows * rows, axis=-1, keepdims=True) + 1e-06)


def delta_local_kernel(key_heads, q_ref, k_ref, v_ref, beta_ref, cum_ref, eff_ref, direct_ref, pack_ref):
    size = q_ref.shape[0]
    repeat = HV // HKD
    row_id = lax.broadcasted_iota(jnp.int32, (size, size), 0)
    col_id = lax.broadcasted_iota(jnp.int32, (size, size), 1)
    lower = row_id >= col_id
    strict = row_id > col_id
    keys, key_key, query_key, query_rows, key_cols, key_rows = [], [], [], [], [], []
    for a in range(key_heads):
        kb = k_ref[:, a * DK : (a + 1) * DK]
        qb = q_ref[:, a * DK : (a + 1) * DK]
        kf, qf = kb.astype(F32), qb.astype(F32)
        k_col = unit_scale(kf)
        q_col = unit_scale(qf) * (1.0 / math.sqrt(DK))
        k_row = jnp.broadcast_to(k_col, (size, size)).T
        keys.append(kb)
        key_cols.append(k_col)
        key_rows.append(k_row[:1])
        query_rows.append(qf * q_col)
        key_key.append(mm_nt(kb, kb) * k_col * k_row)
        query_key.append(mm_nt(qb, kb) * q_col * k_row)
    heads = range(key_heads * repeat)
    ratio, near, inverse, cum_cols = [], [], [], []
    for h in heads:
        cum = cum_ref[h : h + 1, :]
        cum_col = column(cum, size)
        spread = jnp.exp(jnp.where(lower, cum_col - cum, -1e30))
        n = jnp.where(strict, column(beta_ref[h : h + 1, :], size) * spread * key_key[h // repeat], 0.0)
        ratio.append(spread)
        near.append(n)
        cum_cols.append(cum_col)
        first = (row_id // 2) == (col_id // 2)
        inverse.append(jnp.where(row_id == col_id, 1.0, jnp.where(first, -n, 0.0)))
    span = 2
    while span < size:
        part = (row_id // (2 * span) == col_id // (2 * span)) & (row_id // span > col_id // span)
        inner = [mm_square(jnp.where(part, near[h], 0.0), inverse[h]) for h in heads]
        inverse = [inverse[h] - mm_square(inverse[h], inner[h]) for h in heads]
        span *= 2
    for h in heads:
        a = h // repeat
        kb = keys[a]
        cum = cum_ref[h : h + 1, :]
        beta = beta_ref[h : h + 1, :]
        vb = v_ref[:, h * DV : (h + 1) * DV]
        left_v = jnp.concatenate(halves(inverse[h] * beta), axis=1)
        left_k = jnp.concatenate(halves(inverse[h] * (beta * jnp.exp(cum) * key_rows[a])), axis=1)
        solved = jnp.concatenate(
            [
                mm(left_v, jnp.concatenate([vb, vb], axis=0)),
                mm(left_k, jnp.concatenate([kb, kb], axis=0)),
            ],
            axis=1,
        )
        mix_high, mix_low = halves(ratio[h] * query_key[a])
        solved_high, solved_low = halves(solved)
        mixed = mm(
            jnp.concatenate([mix_high, mix_low], axis=1),
            jnp.concatenate([solved_high, solved_high], axis=0),
        ) + mm(mix_high, solved_low)
        direct_ref[h] = mixed[:, :DV]
        cum_col = cum_cols[h][:, :1]
        eff_ref[h] = jnp.exp(cum_col) * query_rows[a] - mixed[:, DV:]
        last = cum[:, size - 1 : size]
        tail = solved * (jnp.exp(last - cum_col) * key_cols[a])
        tail_high, tail_low = halves(tail)
        carry = mm_tn(
            jnp.concatenate([tail_high, tail_low], axis=0), jnp.concatenate([kb, kb], axis=0)
        )
        pack_ref[h, : DV + DK, :] = carry.astype(BF16)
        kept = jnp.broadcast_to(jnp.exp(last), (8, DK))
        kept_high = kept.astype(BF16).astype(F32)
        pack_ref[h, DV + DK :, :] = jnp.concatenate([kept_high, kept - kept_high], axis=0).astype(BF16)


def delta_local(delta_query, delta_key, delta_value, beta, cumulative):
    size = delta_query.shape[0]
    key_heads = 4
    heads = key_heads * (HV // HKD)
    return pl.pallas_call(
        functools.partial(delta_local_kernel, key_heads),
        grid=(HKD // key_heads,),
        in_specs=[
            pl.BlockSpec((size, key_heads * DK), lambda i: (0, i)),
            pl.BlockSpec((size, key_heads * DK), lambda i: (0, i)),
            pl.BlockSpec((size, heads * DV), lambda i: (0, i)),
            pl.BlockSpec((heads, size), lambda i: (i, 0)),
            pl.BlockSpec((heads, size), lambda i: (i, 0)),
        ],
        out_specs=[
            pl.BlockSpec((heads, size, DK), lambda i: (i, 0, 0)),
            pl.BlockSpec((heads, size, DV), lambda i: (i, 0, 0)),
            pl.BlockSpec((heads, PACK, DK), lambda i: (i, 0, 0)),
        ],
        out_shape=[
            jax.ShapeDtypeStruct((HV, size, DK), F32),
            jax.ShapeDtypeStruct((HV, size, DV), F32),
            jax.ShapeDtypeStruct((HV, PACK, DK), BF16),
        ],
        compiler_params=pltpu.CompilerParams(vmem_limit_bytes=VMEM),
        cost_estimate=pl.CostEstimate(
            flops=60_000_000_000, bytes_accessed=12_000_000, transcendentals=1_000_000
        ),
        name="delta_local",
    )(delta_query, delta_key, delta_value, beta, cumulative)


def delta_finish_kernel(heads, pack_ref, eff_ref, direct_ref, gate_ref, gain_ref, out_ref, state_ref):
    index = lax.axis_index("ctx")
    state_ref[...] = jnp.zeros_like(state_ref)

    def lap(k, unused):
        for h in range(heads):
            state = state_ref[h]
            new = pack_ref[k, h, :DV, :].astype(F32)
            change = pack_ref[k, h, DV : DV + DK, :]
            kept = pack_ref[k, h, DV + DK :, :].astype(F32)
            kept = kept[:1] + kept[8:9]
            moved = mm(
                jnp.concatenate(halves(state), axis=1), jnp.concatenate([change, change], axis=0)
            )
            state_ref[h] = kept * state - moved + new
        return unused

    lax.fori_loop(0, index, lap, 0)
    for h in range(heads):
        state_high, state_low = halves(state_ref[h])
        eff_high, eff_low = halves(eff_ref[h])
        rows = (
            mm_nt(
                jnp.concatenate([eff_high, eff_low], axis=1),
                jnp.concatenate([state_high, state_high], axis=1),
            )
            + mm_nt(eff_high, state_low)
            + direct_ref[h]
        )
        scale = lax.rsqrt(jnp.mean(rows * rows, axis=-1, keepdims=True) + 1e-06)
        gate = gate_ref[:, h * DV : (h + 1) * DV].astype(F32)
        gated = rows * scale * gain_ref[...] * (gate / (1.0 + jnp.exp(-gate)))
        out_ref[:, h * DV : (h + 1) * DV] = gated.astype(BF16)


def delta_finish(packs, eff, direct, gate, gain):
    size = gate.shape[0]
    heads = 4
    count = packs.shape[0]
    return pl.pallas_call(
        functools.partial(delta_finish_kernel, heads),
        grid=(HV // heads,),
        in_specs=[
            pl.BlockSpec((count, heads, PACK, DK), lambda i: (0, i, 0, 0)),
            pl.BlockSpec((heads, size, DK), lambda i: (i, 0, 0)),
            pl.BlockSpec((heads, size, DV), lambda i: (i, 0, 0)),
            pl.BlockSpec((size, heads * DV), lambda i: (0, i)),
            pl.BlockSpec((1, DV), lambda i: (0, 0)),
        ],
        out_specs=pl.BlockSpec((size, heads * DV), lambda i: (0, i)),
        out_shape=jax.ShapeDtypeStruct((size, HV * DV), BF16),
        scratch_shapes=[pltpu.VMEM((heads, DV, DK), F32)],
        compiler_params=pltpu.CompilerParams(vmem_limit_bytes=VMEM),
        cost_estimate=pl.CostEstimate(
            flops=20_000_000_000, bytes_accessed=24_000_000, transcendentals=1_000_000
        ),
        name="delta_finish",
    )(packs, eff, direct, gate, gain)


def attention_kernel(heads, q_ref, k_old_ref, v_old_ref, k_ref, v_ref, gate_ref, out_ref):
    size = q_ref.shape[0]
    row_id = lax.broadcasted_iota(jnp.int32, (size, size), 0)
    col_id = lax.broadcasted_iota(jnp.int32, (size, size), 1)
    first = jnp.where(lax.axis_index("ctx") > 0, 0, size)
    seen_old = col_id > row_id + first
    seen = col_id <= row_id
    k_all = jnp.concatenate([k_old_ref[...], k_ref[...]], axis=0)
    v_all = jnp.concatenate([v_old_ref[...], v_ref[...]], axis=0)
    visible = jnp.concatenate([seen_old, seen], axis=1)
    for h in range(heads):
        part = slice(h * HEAD_WIDTH, (h + 1) * HEAD_WIDTH)
        scores = mm_nt(q_ref[:, part], k_all) * (1.0 / math.sqrt(HEAD_WIDTH))
        scores = jnp.where(visible, scores, -jnp.inf)
        lifted = jnp.exp(scores - jnp.max(scores, axis=-1, keepdims=True))
        probs = (lifted / jnp.sum(lifted, axis=-1, keepdims=True)).astype(BF16)
        gate = gate_ref[:, part].astype(F32)
        out_ref[:, part] = (mm(probs, v_all) / (1.0 + jnp.exp(-gate))).astype(BF16)


def window_attention(query, previous, key_value, gate):
    size = query.shape[0]
    heads = 4
    per_group = QUERY_HEADS // KEY_VALUE_HEADS // heads
    wide = pl.BlockSpec((size, heads * HEAD_WIDTH), lambda i: (0, i))
    key = pl.BlockSpec((size, HEAD_WIDTH), lambda i: (0, i // per_group))
    value = pl.BlockSpec((size, HEAD_WIDTH), lambda i: (0, KEY_VALUE_HEADS + i // per_group))
    return pl.pallas_call(
        functools.partial(attention_kernel, heads),
        grid=(QUERY_HEADS // heads,),
        in_specs=[wide, key, value, key, value, wide],
        out_specs=wide,
        out_shape=jax.ShapeDtypeStruct(query.shape, BF16),
        compiler_params=pltpu.CompilerParams(vmem_limit_bytes=VMEM),
        cost_estimate=pl.CostEstimate(
            flops=8_000_000_000, bytes_accessed=4_000_000, transcendentals=1_000_000
        ),
        name="window_attention",
    )(query, previous, previous, key_value, key_value, gate)


def expert_kernel(x_ref, weight_ref, gate_ref, up_ref, down_ref, out_ref):
    rows = x_ref[...]
    gate = mm(rows, gate_ref[0])
    hidden = (gate / (1.0 + jnp.exp(-gate)) * mm(rows, up_ref[0])).astype(BF16)
    result = mm(hidden, down_ref[0]).astype(BF16).astype(F32)
    out_ref[...] = (result * weight_ref[...]).astype(BF16)


def expert_rows(tokens, weights, w_gate, w_up, w_down):
    count, width = tokens.shape
    hidden = w_gate.shape[2]
    tile = 512
    return pl.pallas_call(
        expert_kernel,
        grid=(count // tile,),
        in_specs=[
            pl.BlockSpec((tile, width), lambda i: (i, 0)),
            pl.BlockSpec((tile, 1), lambda i: (i, 0)),
            pl.BlockSpec((1, width, hidden), lambda i: (0, 0, 0)),
            pl.BlockSpec((1, width, hidden), lambda i: (0, 0, 0)),
            pl.BlockSpec((1, hidden, width), lambda i: (0, 0, 0)),
        ],
        out_specs=pl.BlockSpec((tile, width), lambda i: (i, 0)),
        out_shape=jax.ShapeDtypeStruct((count, width), BF16),
        compiler_params=pltpu.CompilerParams(vmem_limit_bytes=VMEM),
        cost_estimate=pl.CostEstimate(
            flops=6 * count * width * hidden,
            bytes_accessed=4 * count * width + 6 * width * hidden,
            transcendentals=count * hidden,
        ),
        name="expert_rows",
    )(tokens, weights, w_gate, w_up, w_down)


def body(
    delta_query,
    delta_key,
    delta_value,
    delta_gate,
    delta_beta,
    delta_decay,
    norm_gain,
    attention_query,
    attention_key_value,
    attention_gate,
    moe_input,
    routes,
    drop_mask,
    route_weights,
    w_gate,
    w_up,
    w_down,
):
    axes = ("seq", "ctx")
    n_ctx = lax.axis_size("ctx")
    n_dev = lax.axis_size("seq") * n_ctx
    me = lax.axis_index("seq") * n_ctx + lax.axis_index("ctx")

    tokens = lax.all_gather(moe_input[0], axes, axis=0, tiled=True)
    kept = drop_mask[0].astype(F32) * route_weights[0]
    chosen = routes[0].T[:, None, :] == jnp.arange(n_dev, dtype=jnp.int32)[None, :, None]
    table = jnp.sum(jnp.where(chosen, kept.T[:, None, :], 0.0), axis=0)
    tables = lax.all_gather(table, axes, axis=0, tiled=False)
    weights = lax.dynamic_index_in_dim(tables, me, axis=1, keepdims=False).reshape(-1, 1)

    previous = lax.ppermute(attention_key_value[0], "ctx", [(i, i + 1) for i in range(n_ctx - 1)])

    places = jnp.arange(delta_decay.shape[-1])
    earlier = places[None, :] <= places[:, None]
    cumulative = jnp.sum(jnp.where(earlier[None], delta_decay[0][:, None, :], 0.0), axis=-1)
    eff, direct, pack = delta_local(
        delta_query[0], delta_key[0], delta_value[0], delta_beta[0], cumulative
    )
    packs = lax.all_gather(pack, "ctx", axis=0, tiled=False)

    parts = expert_rows(tokens, weights, w_gate, w_up, w_down)
    moe_out = lax.psum_scatter(parts, axes, scatter_dimension=0, tiled=True)

    attn_out = window_attention(attention_query[0], previous, attention_key_value[0], attention_gate[0])
    delta_out = delta_finish(packs, eff, direct, delta_gate[0], norm_gain[None])
    return (delta_out[None], attn_out[None], moe_out[None])


def solution(mesh):
    placed = (
        P("seq", "ctx", None),
        P("seq", "ctx", None),
        P("seq", "ctx", None),
        P("seq", "ctx", None),
        P("seq", None, "ctx"),
        P("seq", None, "ctx"),
        P(),
        P("seq", "ctx", None),
        P("seq", "ctx", None),
        P("seq", "ctx", None),
        P("seq", "ctx", None),
        P("seq", "ctx", None),
        P("seq", "ctx", None),
        P("seq", "ctx", None),
        P(("seq", "ctx"), None, None),
        P(("seq", "ctx"), None, None),
        P(("seq", "ctx"), None, None),
    )
    return jax.shard_map(
        body,
        mesh=mesh,
        in_specs=placed,
        out_specs=(P("seq", "ctx", None), P("seq", "ctx", None), P("seq", "ctx", None)),
        check_vma=False,
    )
```
